1024 devices in a mesh: dp: 64 (over z, y_lo), mp: 4 (over x), blk: 4 (over y_hi, core).
Axes of the slice: x: 4, y: 4 (y_hi: 2, y_lo: 2; y = y_hi * 2 + y_lo), z: 32, core: 2. Of those that a mesh axis runs over, the one named last changes fastest.
Arguments:
- activations: bfloat16 [98304, 2560], P('dp', 'blk'), may hold values from -13 to 13
- cotangent: bfloat16 [98304, 2560], P('dp', 'mp'), may hold values from -13 to 13
Outputs:
- update: float32 [4, 640, 2560], P('blk', 'dp', 'mp')
The draws below stay inside these ranges and needn't reach their ends.
All inputs are finite; a program needn't handle non-finite values.
Results may differ from the reference program's by a relative error of at most 0.007.
Values may be sent and summed in bfloat16 or wider, within the bound.
No kernel may reach another device: no remote copies, remote signals or barrier semaphores. Data moves between devices by JAX's collectives and lax.ppermute only.
A program may use at most 32 MiB of HBM per device.

```python
import math
import jax
import jax.numpy as jnp
from jax import lax

BLOCK = 640
TOKENS = 98304
IN_WIN = 2560
OUT_WIN = 2560
N_MP = 4
N_BLK = 4


def feature_scales(key, extent, lower, upper):
    position = (jnp.arange(extent) % BLOCK).astype(jnp.float32) / BLOCK
    spread = jax.random.uniform(key, (extent,), dtype=jnp.float32)
    mixed = 0.6 * position + 0.4 * spread
    return jnp.exp(jnp.log(lower) + (jnp.log(upper) - jnp.log(lower)) * mixed)


def draw_activations(key, part):
    key = jax.random.fold_in(key, 11)
    first_key, second_key = jax.random.split(key, 2)
    scales = feature_scales(first_key, IN_WIN, 0.32, 3.2)
    entries = jnp.clip(jax.random.normal(second_key, (TOKENS, IN_WIN), dtype=jnp.float32), -4.0, 4.0)
    return (entries * scales).astype(jnp.bfloat16)


def draw_cotangent(key, part):
    key = jax.random.fold_in(key, 12)
    first_key, second_key = jax.random.split(key, 2)
    scales = feature_scales(first_key, OUT_WIN, 0.32, 3.2)
    entries = jnp.clip(jax.random.normal(second_key, (TOKENS, OUT_WIN), dtype=jnp.float32), -4.0, 4.0)
    return (entries * scales).astype(jnp.bfloat16)


def setup_inputs(seed: int = 0) -> dict:
    arg_keys = jax.random.split(jax.random.key(seed), 3)
    activations = draw_activations(jax.random.fold_in(arg_keys[2], 71), 0)
    cotangent = draw_cotangent(jax.random.fold_in(arg_keys[2], 71), 0)
    return {"activations": activations, "cotangent": cotangent}


ridge_shift = 0.05
tiny_shift = 1e-12

def inverse_root(statistic):
    highest = lax.Precision.HIGHEST
    extent = statistic.shape[0]
    identity = jnp.eye(extent, dtype=jnp.float32)
    frobenius = jnp.sqrt(jnp.sum(statistic * statistic) + tiny_shift)
    shifted = statistic / frobenius + ridge_shift * identity
    squared = jnp.dot(shifted, shifted, precision=highest, preferred_element_type=jnp.float32)
    factor = (5.0 * identity - shifted) / 4.0
    factor_two = (25.0 * identity - 10.0 * shifted + squared) / 16.0
    factor_four = jnp.dot(factor_two, factor_two, precision=highest, preferred_element_type=jnp.float32)
    factor_shifted = (5.0 * shifted - squared) / 4.0
    product = jnp.dot(factor_four, factor_shifted, precision=highest, preferred_element_type=jnp.float32)
    return ((5.0 * factor - product) / 4.0).astype(jnp.bfloat16)

def reference(activations, cotangent):
    summed = lax.dot_general(activations, cotangent, (((0,), (0,)), ((), ())), preferred_element_type=jnp.float32)
    gradient = (summed * (1.0 / math.sqrt(TOKENS))).astype(jnp.bfloat16)
    row_stack = []
    for row_block in range(N_BLK):
        pieces = []
        for col_block in range(N_MP):
            block_tile = gradient[row_block * BLOCK:(row_block + 1) * BLOCK, col_block * BLOCK:(col_block + 1) * BLOCK]
            left_stat = lax.dot_general(block_tile, block_tile, (((1,), (1,)), ((), ())), preferred_element_type=jnp.float32)
            right_stat = lax.dot_general(block_tile, block_tile, (((0,), (0,)), ((), ())), preferred_element_type=jnp.float32)
            left_root = inverse_root(left_stat)
            right_root = inverse_root(right_stat)
            left_part = jnp.dot(left_root, block_tile, preferred_element_type=jnp.float32).astype(jnp.bfloat16)
            direction = jnp.dot(left_part, right_root, preferred_element_type=jnp.float32)
            widened = block_tile.astype(jnp.float32)
            gradient_norm = jnp.sum(widened * widened)
            direction_norm = jnp.sum(direction * direction)
            pieces.append(direction * jnp.sqrt(gradient_norm / (direction_norm + tiny_shift)))
        row_stack.append(jnp.concatenate(pieces, axis=1))
    return jnp.stack(row_stack, axis=0)
```

```python
import math

import jax
import jax.numpy as jnp
import numpy as np
from jax import lax
from jax.experimental import pallas as pl
from jax.experimental.pallas import tpu as pltpu
from jax.sharding import PartitionSpec as P

ridge_shift = 0.05
tiny_shift = 1e-12
chunk = 128


def root_coefficients():
    poly = np.polynomial.Polynomial
    shifted = poly([ridge_shift, 1.0])
    factor = (5.0 - shifted) / 4.0
    return [float(c) for c in ((5.0 * factor - factor**5 * shifted) / 4.0).coef]


def precondition_kernel(
    start_ref, g_ref, out_ref, stat, one, two, two_wide, three, mixed, base, wide, narrow, direction
):
    q = root_coefficients()
    extent = g_ref.shape[0]
    slices = [pl.ds(i * chunk, chunk) for i in range(extent // chunk)]

    def product(left, right):
        return jnp.dot(left, right, preferred_element_type=jnp.float32)

    total = jnp.float32(0.0)
    for rows in slices:
        part = lax.dot_general(
            g_ref[:, rows], g_ref[...], (((0,), (0,)), ((), ())), preferred_element_type=jnp.float32
        )
        stat[rows, :] = part
        total += jnp.sum(part * part)
    inverse = 1.0 / jnp.sqrt(total + tiny_shift)
    for rows in slices:
        part = stat[rows, :] * inverse
        stat[rows, :] = part
        one[rows, :] = part.astype(jnp.bfloat16)
    for rows in slices:
        part = product(one[rows, :], one[...])
        two_wide[rows, :] = part
        two[rows, :] = part.astype(jnp.bfloat16)
    for rows in slices:
        cubed = product(one[rows, :], two[...])
        first, second = stat[rows, :], two_wide[rows, :]
        three[rows, :] = cubed.astype(jnp.bfloat16)
        base[rows, :] = q[1] * first + q[2] * second + q[3] * cubed
        mixed[rows, :] = (q[4] * first + q[5] * second + q[6] * cubed).astype(jnp.bfloat16)
    for rows in slices:
        part = base[rows, :] + product(three[rows, :], mixed[...])
        wide[rows, :] = part
        narrow[rows, :] = part.astype(jnp.bfloat16)
    for rows in slices:
        part = (2.0 * q[0]) * wide[rows, :] + product(narrow[rows, :], narrow[...])
        one[rows, :] = part.astype(jnp.bfloat16)
    gradient_norm, direction_norm = jnp.float32(0.0), jnp.float32(0.0)
    for rows in slices:
        widened = g_ref[rows, :].astype(jnp.float32)
        part = (q[0] * q[0]) * widened + product(g_ref[rows, :], one[...])
        direction[rows, :] = part
        gradient_norm += jnp.sum(widened * widened)
        direction_norm += jnp.sum(part * part)
    scale = jnp.sqrt(gradient_norm / (direction_norm + tiny_shift))
    for i in range(out_ref.shape[0]):
        out_ref[pl.ds(i, 1), :] = direction[pl.ds(start_ref[0] + i, 1), :] * scale


def precondition(gradient, start, slab_rows):
    extent = gradient.shape[0]
    square = (extent, extent)
    f32, bf16 = pltpu.VMEM(square, jnp.float32), pltpu.VMEM(square, jnp.bfloat16)
    return pl.pallas_call(
        precondition_kernel,
        out_shape=jax.ShapeDtypeStruct((slab_rows, extent), jnp.float32),
        in_specs=[
            pl.BlockSpec(memory_space=pltpu.SMEM),
            pl.BlockSpec(memory_space=pltpu.VMEM),
        ],
        out_specs=pl.BlockSpec(memory_space=pltpu.VMEM),
        scratch_shapes=[f32, bf16, bf16, f32, bf16, bf16, f32, f32, bf16, f32],
        compiler_params=pltpu.CompilerParams(vmem_limit_bytes=40 * 1024 * 1024),
        cost_estimate=pl.CostEstimate(
            flops=12 * extent**3, bytes_accessed=2 * extent * extent, transcendentals=2
        ),
    )(start, gradient)


def stage_groups(count):
    near = [[4 * k + r for r in range(4)] for k in range(count // 4)]
    middle = [[16 * b + 4 * j + r for j in range(4)] for b in range(count // 16) for r in range(4)]
    far = [[16 * b + c for b in range(count // 16)] for c in range(16)]
    return near, middle, far


def exchange(parts, groups):
    return lax.all_to_all(parts, "dp", 0, 0, axis_index_groups=groups)


def summed(parts):
    return jnp.sum(parts.astype(jnp.float32), axis=0).astype(jnp.bfloat16)


def spread(part, groups):
    count = len(groups[0])
    return exchange(jnp.broadcast_to(part[None], (count,) + part.shape), groups)


def per_device(activations, cotangent):
    dp_count = lax.axis_size("dp")
    dp_index = lax.axis_index("dp")
    extent = cotangent.shape[1]
    slab_rows = extent // dp_count
    scaling = 1.0 / math.sqrt(activations.shape[0] * dp_count)
    near, middle, far = stage_groups(dp_count)
    with jax.named_scope("product"):
        product = lax.dot_general(
            activations, cotangent, (((0,), (0,)), ((), ())), preferred_element_type=jnp.float32
        )
        part = (product * scaling).astype(jnp.bfloat16)
    with jax.named_scope("near_sum"):
        part = summed(exchange(part.reshape(4, extent // 4, extent), near))
    with jax.named_scope("middle_sum"):
        part = summed(exchange(part.reshape(4, extent // 16, extent), middle))
    with jax.named_scope("far_sum"):
        part = summed(spread(part, far))
    with jax.named_scope("middle_gather"):
        part = spread(part, middle).reshape(extent // 4, extent)
    with jax.named_scope("near_gather"):
        gradient = spread(part, near).reshape(extent, extent)
    with jax.named_scope("precondition"):
        start = jnp.reshape(dp_index * slab_rows, (1,)).astype(jnp.int32)
        return precondition(gradient, start, slab_rows)[None]


def solution(mesh):
    placed = (P("dp", "blk"), P("dp", "mp"))
    return jax.shard_map(
        per_device, mesh=mesh, in_specs=placed, out_specs=P("blk", "dp", "mp"), check_vma=False
    )
```

```python
import math

import jax
import jax.numpy as jnp
import numpy as np
from jax import lax
from jax.experimental import pallas as pl
from jax.experimental.pallas import tpu as pltpu
from jax.sharding import PartitionSpec as P

ridge_shift = 0.05
tiny_shift = 1e-12
chunk = 640
axes = ("dp", "mp", "blk")
core_shift = 9
stage_bits = (((0, 1), (2, 3), (4, 5)), ((0, 1), (2, 3), (4, 5)))


def root_coefficients():
    poly = np.polynomial.Polynomial
    shifted = poly([ridge_shift, 1.0])
    factor = (5.0 - shifted) / 4.0
    return [float(c) for c in ((5.0 * factor - factor**5 * shifted) / 4.0).coef]


def folded(part):
    return jnp.sum(part.reshape(part.shape[0] // 8, 8, part.shape[1]), axis=0)


def precondition_kernel(
    start_ref, g_ref, out_ref, stat, one, two, two_wide, three, mixed, base, wide, narrow, direction
):
    q = root_coefficients()
    extent = g_ref.shape[0]
    slices = [pl.ds(i * chunk, chunk) for i in range(extent // chunk)]

    def product(left, right):
        return jnp.dot(left, right, preferred_element_type=jnp.float32)

    total = jnp.zeros((8, extent), jnp.float32)
    for rows in slices:
        part = lax.dot_general(
            g_ref[:, rows], g_ref[...], (((0,), (0,)), ((), ())), preferred_element_type=jnp.float32
        )
        stat[rows, :] = part
        one[rows, :] = part.astype(jnp.bfloat16)
        total += folded(part * part)
    inverse = 1.0 / jnp.sqrt(jnp.sum(total) + tiny_shift)
    for rows in slices:
        part = product(one[rows, :], one[...]) * (inverse * inverse)
        two_wide[rows, :] = part
        two[rows, :] = part.astype(jnp.bfloat16)
    for rows in slices:
        cubed = product(one[rows, :], two[...]) * inverse
        first, second = stat[rows, :] * inverse, two_wide[rows, :]
        three[rows, :] = cubed.astype(jnp.bfloat16)
        base[rows, :] = q[1] * first + q[2] * second + q[3] * cubed
        mixed[rows, :] = (q[4] * first + q[5] * second + q[6] * cubed).astype(jnp.bfloat16)
    for rows in slices:
        part = base[rows, :] + product(three[rows, :], mixed[...])
        wide[rows, :] = part
        narrow[rows, :] = part.astype(jnp.bfloat16)
    for rows in slices:
        part = (2.0 * q[0]) * wide[rows, :] + product(narrow[rows, :], narrow[...])
        one[rows, :] = part.astype(jnp.bfloat16)
    gradient_norm = jnp.zeros((8, extent), jnp.float32)
    direction_norm = jnp.zeros((8, extent), jnp.float32)
    for rows in slices:
        widened = g_ref[rows, :].astype(jnp.float32)
        part = (q[0] * q[0]) * widened + product(g_ref[rows, :], one[...])
        direction[rows, :] = part
        gradient_norm += folded(widened * widened)
        direction_norm += folded(part * part)
    scale = jnp.sqrt(jnp.sum(gradient_norm) / (jnp.sum(direction_norm) + tiny_shift))
    for i in range(out_ref.shape[0]):
        out_ref[i] = direction[pl.ds(start_ref[0] + i, 1), :] * scale


def precondition(gradient, start, slab_rows):
    extent = gradient.shape[0]
    square = (extent, extent)
    f32, bf16 = pltpu.VMEM(square, jnp.float32), pltpu.VMEM(square, jnp.bfloat16)
    return pl.pallas_call(
        precondition_kernel,
        out_shape=jax.ShapeDtypeStruct((slab_rows, 1, extent), jnp.float32),
        in_specs=[
            pl.BlockSpec(memory_space=pltpu.SMEM),
            pl.BlockSpec(memory_space=pltpu.VMEM),
        ],
        out_specs=pl.BlockSpec(memory_space=pltpu.VMEM),
        scratch_shapes=[f32, bf16, bf16, f32, bf16, bf16, f32, f32, bf16, f32],
        compiler_params=pltpu.CompilerParams(vmem_limit_bytes=40 * 1024 * 1024),
        cost_estimate=pl.CostEstimate(
            flops=12 * extent**3, bytes_accessed=2 * extent * extent, transcendentals=2
        ),
    )(start, gradient)


def stage_groups():
    count, n_mp, n_blk = (lax.axis_size(axis) for axis in axes)
    rings = count // 2

    def placed(stage):
        groups = []
        for mp in range(n_mp):
            for blk in range(n_blk):
                core = blk % 2
                low, high = (1 << bit for bit in stage_bits[core][stage])
                for base in range(count):
                    if base & (low | high):
                        continue
                    members = [base, base | low, base | high, base | low | high]
                    groups.append([
                        (((v // 2 + core_shift * core) % rings * 2 + v % 2) * n_mp + mp) * n_blk + blk
                        for v in members
                    ])
        return groups

    return [placed(stage) for stage in range(3)]


def exchange(parts, groups):
    return lax.all_to_all(parts, axes, 0, 0, axis_index_groups=groups)


def summed(parts):
    return jnp.sum(parts.astype(jnp.float32), axis=0).astype(jnp.bfloat16)


def spread(part, groups):
    count = len(groups[0])
    return exchange(jnp.broadcast_to(part[None], (count,) + part.shape), groups)


def per_device(activations, cotangent):
    dp_count = lax.axis_size("dp")
    dp_index = lax.axis_index("dp")
    extent = cotangent.shape[1]
    slab_rows = extent // dp_count
    scaling = 1.0 / math.sqrt(activations.shape[0] * dp_count)
    near, middle, far = stage_groups()
    with jax.named_scope("product"):
        product = lax.dot_general(
            activations, cotangent, (((0,), (0,)), ((), ())), preferred_element_type=jnp.float32
        )
        part = (product * scaling).astype(jnp.bfloat16)
    with jax.named_scope("near_sum"):
        part = summed(exchange(part.reshape(4, extent // 4, extent), near))
    with jax.named_scope("middle_sum"):
        part = summed(exchange(part.reshape(4, extent // 16, extent), middle))
    with jax.named_scope("far_sum"):
        part = summed(lax.all_gather(part, axes, axis_index_groups=far))
    with jax.named_scope("middle_gather"):
        part = spread(part, middle).reshape(extent // 4, extent)
    with jax.named_scope("near_gather"):
        gradient = spread(part, near).reshape(extent, extent)
    with jax.named_scope("precondition"):
        start = jnp.reshape(dp_index * slab_rows, (1,)).astype(jnp.int32)
        return jnp.transpose(precondition(gradient, start, slab_rows), (1, 0, 2))


def solution(mesh):
    placed = (P("dp", "blk"), P("dp", "mp"))
    return jax.shard_map(
        per_device, mesh=mesh, in_specs=placed, out_specs=P("blk", "dp", "mp"), check_vma=False
    )
```

```python
import math

import jax
import jax.numpy as jnp
import numpy as np
from jax import lax
from jax.experimental import pallas as pl
from jax.experimental.pallas import tpu as pltpu
from jax.sharding import PartitionSpec as P

ridge_shift = 0.05
tiny_shift = 1e-12
chunk = 640
axes = ("dp", "mp", "blk")
core_shift = 9
stage_bits = (((0, 1), (2, 3), (4, 5)), ((0, 1), (2, 3), (4, 5)))


def root_coefficients():
    poly = np.polynomial.Polynomial
    shifted = poly([ridge_shift, 1.0])
    factor = (5.0 - shifted) / 4.0
    return [float(c) for c in ((5.0 * factor - factor**5 * shifted) / 4.0).coef]


def folded(part):
    return jnp.sum(part.reshape(part.shape[0] // 8, 8, part.shape[1]), axis=0)


def precondition_kernel(
    g_ref, out_ref, stat, one, two, two_wide, three, mixed, base, wide, narrow, direction
):
    q = root_coefficients()
    extent = g_ref.shape[0]
    slices = [pl.ds(i * chunk, chunk) for i in range(extent // chunk)]

    def product(left, right):
        return jnp.dot(left, right, preferred_element_type=jnp.float32)

    total = jnp.zeros((8, extent), jnp.float32)
    for rows in slices:
        part = lax.dot_general(
            g_ref[:, rows], g_ref[...], (((0,), (0,)), ((), ())), preferred_element_type=jnp.float32
        )
        stat[rows, :] = part
        one[rows, :] = part.astype(jnp.bfloat16)
        total += folded(part * part)
    inverse = 1.0 / jnp.sqrt(jnp.sum(total) + tiny_shift)
    for rows in slices:
        part = product(one[rows, :], one[...]) * (inverse * inverse)
        two_wide[rows, :] = part
        two[rows, :] = part.astype(jnp.bfloat16)
    for rows in slices:
        cubed = product(one[rows, :], two[...]) * inverse
        first, second = stat[rows, :] * inverse, two_wide[rows, :]
        three[rows, :] = cubed.astype(jnp.bfloat16)
        base[rows, :] = q[1] * first + q[2] * second + q[3] * cubed
        mixed[rows, :] = (q[4] * first + q[5] * second + q[6] * cubed).astype(jnp.bfloat16)
    for rows in slices:
        part = base[rows, :] + product(three[rows, :], mixed[...])
        wide[rows, :] = part
        narrow[rows, :] = part.astype(jnp.bfloat16)
    for rows in slices:
        part = (2.0 * q[0]) * wide[rows, :] + product(narrow[rows, :], narrow[...])
        one[rows, :] = part.astype(jnp.bfloat16)
    gradient_norm = jnp.zeros((8, extent), jnp.float32)
    direction_norm = jnp.zeros((8, extent), jnp.float32)
    for rows in slices:
        widened = g_ref[rows, :].astype(jnp.float32)
        part = (q[0] * q[0]) * widened + product(g_ref[rows, :], one[...])
        direction[rows, :] = part
        gradient_norm += folded(widened * widened)
        direction_norm += folded(part * part)
    start = lax.axis_index("dp") * out_ref.shape[0]
    scale = jnp.sqrt(jnp.sum(gradient_norm) / (jnp.sum(direction_norm) + tiny_shift))
    for i in range(out_ref.shape[0]):
        out_ref[i] = direction[pl.ds(start + i, 1), :] * scale


def precondition(gradient, slab_rows):
    extent = gradient.shape[0]
    square = (extent, extent)
    f32, bf16 = pltpu.VMEM(square, jnp.float32), pltpu.VMEM(square, jnp.bfloat16)
    return pl.pallas_call(
        precondition_kernel,
        out_shape=jax.ShapeDtypeStruct((slab_rows, 1, extent), jnp.float32),
        in_specs=[
            pl.BlockSpec(memory_space=pltpu.VMEM),
        ],
        out_specs=pl.BlockSpec(memory_space=pltpu.VMEM),
        scratch_shapes=[f32, bf16, bf16, f32, bf16, bf16, f32, f32, bf16, f32],
        compiler_params=pltpu.CompilerParams(vmem_limit_bytes=40 * 1024 * 1024),
        cost_estimate=pl.CostEstimate(
            flops=12 * extent**3, bytes_accessed=2 * extent * extent, transcendentals=2
        ),
    )(gradient)


def stage_groups():
    count, n_mp, n_blk = (lax.axis_size(axis) for axis in axes)
    rings = count // 2

    def placed(stage):
        groups = []
        for mp in range(n_mp):
            for blk in range(n_blk):
                core = blk % 2
                low, high = (1 << bit for bit in stage_bits[core][stage])
                for base in range(count):
                    if base & (low | high):
                        continue
                    members = [base, base | low, base | high, base | low | high]
                    groups.append([
                        (((v // 2 + core_shift * core) % rings * 2 + v % 2) * n_mp + mp) * n_blk + blk
                        for v in members
                    ])
        return groups

    return [placed(stage) for stage in range(3)]


def exchange(parts, groups):
    return lax.all_to_all(parts, axes, 0, 0, axis_index_groups=groups)


def summed(parts):
    return jnp.sum(parts.astype(jnp.float32), axis=0).astype(jnp.bfloat16)


def spread(part, groups):
    count = len(groups[0])
    return exchange(jnp.broadcast_to(part[None], (count,) + part.shape), groups)


def per_device(activations, cotangent):
    dp_count = lax.axis_size("dp")
    extent = cotangent.shape[1]
    slab_rows = extent // dp_count
    scaling = 1.0 / math.sqrt(activations.shape[0] * dp_count)
    near, middle, far = stage_groups()
    with jax.named_scope("product"):
        product = lax.dot_general(
            activations, cotangent, (((0,), (0,)), ((), ())), preferred_element_type=jnp.float32
        )
        part = (product * scaling).astype(jnp.bfloat16)
    with jax.named_scope("near_sum"):
        part = summed(exchange(part.reshape(4, extent // 4, extent), near))
    with jax.named_scope("middle_sum"):
        part = summed(exchange(part.reshape(4, extent // 16, extent), middle))
    with jax.named_scope("far_sum"):
        part = summed(lax.all_gather(part, axes, axis_index_groups=far))
    with jax.named_scope("middle_gather"):
        part = spread(part, middle).reshape(extent // 4, extent)
    with jax.named_scope("near_gather"):
        gradient = spread(part, near).reshape(extent, extent)
    with jax.named_scope("precondition"):
        return jnp.transpose(precondition(gradient, slab_rows), (1, 0, 2))


def solution(mesh):
    placed = (P("dp", "blk"), P("dp", "mp"))
    return jax.shard_map(
        per_device, mesh=mesh, in_specs=placed, out_specs=P("blk", "dp", "mp"), check_vma=False
    )
```

```python
import functools
import math

import jax
import jax.numpy as jnp
import numpy as np
from jax import lax
from jax.experimental import pallas as pl
from jax.experimental.pallas import tpu as pltpu
from jax.sharding import PartitionSpec as P

ridge_shift = 0.05
tiny_shift = 1e-12
chunk = 640
axes = ("dp", "mp", "blk")
core_shifts = (30, 27)


def root_coefficients():
    poly = np.polynomial.Polynomial
    shifted = poly([ridge_shift, 1.0])
    factor = (5.0 - shifted) / 4.0
    return [float(c) for c in ((5.0 * factor - factor**5 * shifted) / 4.0).coef]


def folded(part):
    return jnp.sum(part.reshape(part.shape[0] // 8, 8, part.shape[1]), axis=0)


def precondition_kernel(
    g_ref, out_ref, stat, one, two, two_wide, three, mixed, base, wide, narrow, direction
):
    q = root_coefficients()
    extent = g_ref.shape[0]
    slices = [pl.ds(i * chunk, chunk) for i in range(extent // chunk)]

    def product(left, right):
        return jnp.dot(left, right, preferred_element_type=jnp.float32)

    total = jnp.zeros((8, extent), jnp.float32)
    for rows in slices:
        part = lax.dot_general(
            g_ref[:, rows], g_ref[...], (((0,), (0,)), ((), ())), preferred_element_type=jnp.float32
        )
        stat[rows, :] = part
        one[rows, :] = part.astype(jnp.bfloat16)
        total += folded(part * part)
    inverse = 1.0 / jnp.sqrt(jnp.sum(total) + tiny_shift)
    for rows in slices:
        part = product(one[rows, :], one[...]) * (inverse * inverse)
        two_wide[rows, :] = part
        two[rows, :] = part.astype(jnp.bfloat16)
    for rows in slices:
        cubed = product(one[rows, :], two[...]) * inverse
        first, second = stat[rows, :] * inverse, two_wide[rows, :]
        three[rows, :] = cubed.astype(jnp.bfloat16)
        base[rows, :] = q[1] * first + q[2] * second + q[3] * cubed
        mixed[rows, :] = (q[4] * first + q[5] * second + q[6] * cubed).astype(jnp.bfloat16)
    for rows in slices:
        part = base[rows, :] + product(three[rows, :], mixed[...])
        wide[rows, :] = part
        narrow[rows, :] = part.astype(jnp.bfloat16)
    for rows in slices:
        part = (2.0 * q[0]) * wide[rows, :] + product(narrow[rows, :], narrow[...])
        one[rows, :] = part.astype(jnp.bfloat16)
    gradient_norm = jnp.zeros((8, extent), jnp.float32)
    direction_norm = jnp.zeros((8, extent), jnp.float32)
    for rows in slices:
        widened = g_ref[rows, :].astype(jnp.float32)
        part = (q[0] * q[0]) * widened + product(g_ref[rows, :], one[...])
        direction[rows, :] = part
        gradient_norm += folded(widened * widened)
        direction_norm += folded(part * part)
    start = lax.axis_index("dp") * out_ref.shape[0]
    scale = jnp.sqrt(jnp.sum(gradient_norm) / (jnp.sum(direction_norm) + tiny_shift))
    for i in range(out_ref.shape[0]):
        out_ref[i] = direction[pl.ds(start + i, 1), :] * scale


def precondition(gradient, slab_rows):
    extent = gradient.shape[0]
    square = (extent, extent)
    f32, bf16 = pltpu.VMEM(square, jnp.float32), pltpu.VMEM(square, jnp.bfloat16)
    return pl.pallas_call(
        precondition_kernel,
        out_shape=jax.ShapeDtypeStruct((slab_rows, 1, extent), jnp.float32),
        in_specs=[
            pl.BlockSpec(memory_space=pltpu.VMEM),
        ],
        out_specs=pl.BlockSpec(memory_space=pltpu.VMEM),
        scratch_shapes=[f32, bf16, bf16, f32, bf16, bf16, f32, f32, bf16, f32],
        compiler_params=pltpu.CompilerParams(vmem_limit_bytes=40 * 1024 * 1024),
        cost_estimate=pl.CostEstimate(
            flops=12 * extent**3, bytes_accessed=2 * extent * extent, transcendentals=2
        ),
    )(gradient)


def flat_index(virtual, mp, blk):
    count, n_mp, n_blk = (lax.axis_size(axis) for axis in axes)
    place = (virtual // 2 + core_shifts[blk % 2]) % (count // 2) * 2 + virtual % 2
    return (place * n_mp + mp) * n_blk + blk


def columns():
    return [(mp, blk) for mp in range(lax.axis_size("mp")) for blk in range(lax.axis_size("blk"))]


def stage_groups(low, high):
    return [
        [flat_index(base | member, mp, blk) for member in (0, low, high, low | high)]
        for mp, blk in columns()
        for base in range(lax.axis_size("dp"))
        if not base & (low | high)
    ]


def far_sum(part):
    count = lax.axis_size("dp")
    links = [
        [(flat_index(source, mp, blk), flat_index(source % 16, mp, blk)) for mp, blk in columns() for source in range(16 * run, 16 * run + 16)]
        for run in range(1, count // 16)
    ]
    total = part.astype(jnp.float32)
    for received in [lax.ppermute(part, axes, link) for link in links]:
        total += received.astype(jnp.float32)
    total = total.astype(jnp.bfloat16)
    returned = [lax.ppermute(total, axes, [(b, a) for a, b in link]) for link in links]
    shift = jnp.where(lax.axis_index("blk") % 2 == 0, core_shifts[0], core_shifts[1])
    first = (lax.axis_index("dp") // 2 - shift) % (count // 2) < 8
    return jnp.where(first, total, functools.reduce(jnp.add, returned))


def exchange(parts, groups):
    return lax.all_to_all(parts, axes, 0, 0, axis_index_groups=groups)


def summed(parts):
    return jnp.sum(parts.astype(jnp.float32), axis=0).astype(jnp.bfloat16)


def spread(part, groups):
    count = len(groups[0])
    return exchange(jnp.broadcast_to(part[None], (count,) + part.shape), groups)


def per_device(activations, cotangent):
    dp_count = lax.axis_size("dp")
    extent = cotangent.shape[1]
    slab_rows = extent // dp_count
    scaling = 1.0 / math.sqrt(activations.shape[0] * dp_count)
    near, middle = stage_groups(1, 2), stage_groups(4, 8)
    with jax.named_scope("product"):
        product = lax.dot_general(
            activations, cotangent, (((0,), (0,)), ((), ())), preferred_element_type=jnp.float32
        )
        part = (product * scaling).astype(jnp.bfloat16)
    with jax.named_scope("near_sum"):
        part = summed(exchange(part.reshape(4, extent // 4, extent), near))
    with jax.named_scope("middle_sum"):
        part = summed(exchange(part.reshape(4, extent // 16, extent), middle))
    with jax.named_scope("far_sum"):
        part = far_sum(part)
    with jax.named_scope("middle_gather"):
        part = spread(part, middle).reshape(extent // 4, extent)
    with jax.named_scope("near_gather"):
        gradient = spread(part, near).reshape(extent, extent)
    with jax.named_scope("precondition"):
        return jnp.transpose(precondition(gradient, slab_rows), (1, 0, 2))


def solution(mesh):
    placed = (P("dp", "blk"), P("dp", "mp"))
    return jax.shard_map(
        per_device, mesh=mesh, in_specs=placed, out_specs=P("blk", "dp", "mp"), check_vma=False
    )
```

```python
import functools
import math

import jax
import jax.numpy as jnp
import numpy as np
from jax import lax
from jax.experimental import pallas as pl
from jax.experimental.pallas import tpu as pltpu
from jax.sharding import PartitionSpec as P

ridge_shift = 0.05
tiny_shift = 1e-12
chunk = 640
axes = ("dp", "mp", "blk")
core_shifts = (0, 27)


def root_coefficients():
    poly = np.polynomial.Polynomial
    shifted = poly([ridge_shift, 1.0])
    factor = (5.0 - shifted) / 4.0
    return [float(c) for c in ((5.0 * factor - factor**5 * shifted) / 4.0).coef]


def folded(part):
    return jnp.sum(part.reshape(part.shape[0] // 8, 8, part.shape[1]), axis=0)


def precondition_kernel(
    g_ref, out_ref, stat, one, two, two_wide, three, mixed, base, wide, narrow, direction
):
    q = root_coefficients()
    extent = g_ref.shape[0]
    slices = [pl.ds(i * chunk, chunk) for i in range(extent // chunk)]

    def product(left, right):
        return jnp.dot(left, right, preferred_element_type=jnp.float32)

    total = jnp.zeros((8, extent), jnp.float32)
    for rows in slices:
        part = lax.dot_general(
            g_ref[:, rows], g_ref[...], (((0,), (0,)), ((), ())), preferred_element_type=jnp.float32
        )
        stat[rows, :] = part
        one[rows, :] = part.astype(jnp.bfloat16)
        total += folded(part * part)
    inverse = 1.0 / jnp.sqrt(jnp.sum(total) + tiny_shift)
    for rows in slices:
        part = product(one[rows, :], one[...]) * (inverse * inverse)
        two_wide[rows, :] = part
        two[rows, :] = part.astype(jnp.bfloat16)
    for rows in slices:
        cubed = product(one[rows, :], two[...]) * inverse
        first, second = stat[rows, :] * inverse, two_wide[rows, :]
        three[rows, :] = cubed.astype(jnp.bfloat16)
        base[rows, :] = q[1] * first + q[2] * second + q[3] * cubed
        mixed[rows, :] = (q[4] * first + q[5] * second + q[6] * cubed).astype(jnp.bfloat16)
    for rows in slices:
        part = base[rows, :] + product(three[rows, :], mixed[...])
        wide[rows, :] = part
        narrow[rows, :] = part.astype(jnp.bfloat16)
    for rows in slices:
        part = (2.0 * q[0]) * wide[rows, :] + product(narrow[rows, :], narrow[...])
        one[rows, :] = part.astype(jnp.bfloat16)
    gradient_norm = jnp.zeros((8, extent), jnp.float32)
    direction_norm = jnp.zeros((8, extent), jnp.float32)
    for rows in slices:
        widened = g_ref[rows, :].astype(jnp.float32)
        part = (q[0] * q[0]) * widened + product(g_ref[rows, :], one[...])
        direction[rows, :] = part
        gradient_norm += folded(widened * widened)
        direction_norm += folded(part * part)
    start = lax.axis_index("dp") * out_ref.shape[0]
    scale = jnp.sqrt(jnp.sum(gradient_norm) / (jnp.sum(direction_norm) + tiny_shift))
    for i in range(out_ref.shape[0]):
        out_ref[i] = direction[pl.ds(start + i, 1), :] * scale


def precondition(gradient, slab_rows):
    extent = gradient.shape[0]
    square = (extent, extent)
    f32, bf16 = pltpu.VMEM(square, jnp.float32), pltpu.VMEM(square, jnp.bfloat16)
    return pl.pallas_call(
        precondition_kernel,
        out_shape=jax.ShapeDtypeStruct((slab_rows, 1, extent), jnp.float32),
        in_specs=[
            pl.BlockSpec(memory_space=pltpu.VMEM),
        ],
        out_specs=pl.BlockSpec(memory_space=pltpu.VMEM),
        scratch_shapes=[f32, bf16, bf16, f32, bf16, bf16, f32, f32, bf16, f32],
        compiler_params=pltpu.CompilerParams(vmem_limit_bytes=40 * 1024 * 1024),
        cost_estimate=pl.CostEstimate(
            flops=12 * extent**3, bytes_accessed=2 * extent * extent, transcendentals=2
        ),
    )(gradient)


def flat_index(virtual, mp, blk):
    count, n_mp, n_blk = (lax.axis_size(axis) for axis in axes)
    place = (virtual // 2 + core_shifts[blk % 2]) % (count // 2) * 2 + virtual % 2
    return (place * n_mp + mp) * n_blk + blk


def columns():
    return [(mp, blk) for mp in range(lax.axis_size("mp")) for blk in range(lax.axis_size("blk"))]


def stage_groups(low, high):
    return [
        [flat_index(base | member, mp, blk) for member in (0, low, high, low | high)]
        for mp, blk in columns()
        for base in range(lax.axis_size("dp"))
        if not base & (low | high)
    ]


def far_sum(part):
    count = lax.axis_size("dp")
    links = [
        [(flat_index(source, mp, blk), flat_index(source % 16, mp, blk)) for mp, blk in columns() for source in range(16 * run, 16 * run + 16)]
        for run in range(1, count // 16)
    ]
    total = part.astype(jnp.float32)
    for received in [lax.ppermute(part, axes, link) for link in links]:
        total += received.astype(jnp.float32)
    total = total.astype(jnp.bfloat16)
    returned = [lax.ppermute(total, axes, [(b, a) for a, b in link]) for link in links]
    shift = jnp.where(lax.axis_index("blk") % 2 == 0, core_shifts[0], core_shifts[1])
    first = (lax.axis_index("dp") // 2 - shift) % (count // 2) < 8
    return jnp.where(first, total, functools.reduce(jnp.add, returned))


def exchange(parts, groups):
    return lax.all_to_all(parts, axes, 0, 0, axis_index_groups=groups)


def summed(parts):
    return jnp.sum(parts.astype(jnp.float32), axis=0).astype(jnp.bfloat16)


def spread(part, groups):
    count = len(groups[0])
    return exchange(jnp.broadcast_to(part[None], (count,) + part.shape), groups)


def per_device(activations, cotangent):
    dp_count = lax.axis_size("dp")
    extent = cotangent.shape[1]
    slab_rows = extent // dp_count
    scaling = 1.0 / math.sqrt(activations.shape[0] * dp_count)
    near, middle = stage_groups(1, 2), stage_groups(4, 8)
    with jax.named_scope("product"):
        product = lax.dot_general(
            activations, cotangent, (((0,), (0,)), ((), ())), preferred_element_type=jnp.float32
        )
        part = (product * scaling).astype(jnp.bfloat16)
    with jax.named_scope("near_sum"):
        part = summed(exchange(part.reshape(4, extent // 4, extent), near))
    with jax.named_scope("middle_sum"):
        part = summed(exchange(part.reshape(4, extent // 16, extent), middle))
    with jax.named_scope("far_sum"):
        part = far_sum(part)
    with jax.named_scope("middle_gather"):
        part = spread(part, middle).reshape(extent // 4, extent)
    with jax.named_scope("near_gather"):
        gradient = spread(part, near).reshape(extent, extent)
    with jax.named_scope("precondition"):
        return jnp.transpose(precondition(gradient, slab_rows), (1, 0, 2))


def solution(mesh):
    placed = (P("dp", "blk"), P("dp", "mp"))
    return jax.shard_map(
        per_device, mesh=mesh, in_specs=placed, out_specs=P("blk", "dp", "mp"), check_vma=False
    )
```

```python
import functools
import math

import jax
import jax.numpy as jnp
import numpy as np
from jax import lax
from jax.experimental import pallas as pl
from jax.experimental.pallas import tpu as pltpu
from jax.sharding import PartitionSpec as P

ridge_shift = 0.05
tiny_shift = 1e-12
chunk = 640
axes = ("dp", "mp", "blk")
core_shifts = (0, 27)


def root_coefficients():
    poly = np.polynomial.Polynomial
    shifted = poly([ridge_shift, 1.0])
    factor = (5.0 - shifted) / 4.0
    return [float(c) for c in ((5.0 * factor - factor**5 * shifted) / 4.0).coef]


def folded(part):
    return jnp.sum(part.reshape(part.shape[0] // 8, 8, part.shape[1]), axis=0)


def precondition_kernel(
    g_ref, out_ref, stat, one, two, two_wide, three, mixed, base, wide, narrow, direction
):
    q = root_coefficients()
    extent = g_ref.shape[0]
    slices = [pl.ds(i * chunk, chunk) for i in range(extent // chunk)]

    def product(left, right):
        return jnp.dot(left, right, preferred_element_type=jnp.float32)

    total = jnp.zeros((8, extent), jnp.float32)
    for rows in slices:
        part = lax.dot_general(
            g_ref[:, rows], g_ref[...], (((0,), (0,)), ((), ())), preferred_element_type=jnp.float32
        )
        stat[rows, :] = part
        one[rows, :] = part.astype(jnp.bfloat16)
        total += folded(part * part)
    inverse = 1.0 / jnp.sqrt(jnp.sum(total) + tiny_shift)
    for rows in slices:
        part = product(one[rows, :], one[...]) * (inverse * inverse)
        two_wide[rows, :] = part
        two[rows, :] = part.astype(jnp.bfloat16)
    for rows in slices:
        cubed = product(one[rows, :], two[...]) * inverse
        first, second = stat[rows, :] * inverse, two_wide[rows, :]
        three[rows, :] = cubed.astype(jnp.bfloat16)
        base[rows, :] = q[1] * first + q[2] * second + q[3] * cubed
        mixed[rows, :] = (q[4] * first + q[5] * second + q[6] * cubed).astype(jnp.bfloat16)
    for rows in slices:
        part = base[rows, :] + product(three[rows, :], mixed[...])
        wide[rows, :] = part
        narrow[rows, :] = part.astype(jnp.bfloat16)
    for rows in slices:
        part = (2.0 * q[0]) * wide[rows, :] + product(narrow[rows, :], narrow[...])
        one[rows, :] = part.astype(jnp.bfloat16)
    gradient_norm = jnp.zeros((8, extent), jnp.float32)
    direction_norm = jnp.zeros((8, extent), jnp.float32)
    for rows in slices:
        widened = g_ref[rows, :].astype(jnp.float32)
        part = (q[0] * q[0]) * widened + product(g_ref[rows, :], one[...])
        direction[rows, :] = part
        gradient_norm += folded(widened * widened)
        direction_norm += folded(part * part)
    start = lax.axis_index("dp") * out_ref.shape[0]
    scale = jnp.sqrt(jnp.sum(gradient_norm) / (jnp.sum(direction_norm) + tiny_shift))
    for i in range(out_ref.shape[0]):
        out_ref[i] = direction[pl.ds(start + i, 1), :] * scale


def precondition(gradient, slab_rows):
    extent = gradient.shape[0]
    square = (extent, extent)
    f32, bf16 = pltpu.VMEM(square, jnp.float32), pltpu.VMEM(square, jnp.bfloat16)
    return pl.pallas_call(
        precondition_kernel,
        out_shape=jax.ShapeDtypeStruct((slab_rows, 1, extent), jnp.float32),
        in_specs=[
            pl.BlockSpec(memory_space=pltpu.VMEM),
        ],
        out_specs=pl.BlockSpec(memory_space=pltpu.VMEM),
        scratch_shapes=[f32, bf16, bf16, f32, bf16, bf16, f32, f32, bf16, f32],
        compiler_params=pltpu.CompilerParams(vmem_limit_bytes=40 * 1024 * 1024),
        cost_estimate=pl.CostEstimate(
            flops=12 * extent**3, bytes_accessed=2 * extent * extent, transcendentals=2
        ),
    )(gradient)


def flat_index(virtual, mp, blk):
    count, n_mp, n_blk = (lax.axis_size(axis) for axis in axes)
    place = (virtual // 2 + core_shifts[blk % 2]) % (count // 2) * 2 + virtual % 2
    return (place * n_mp + mp) * n_blk + blk


def columns():
    return [(mp, blk) for mp in range(lax.axis_size("mp")) for blk in range(lax.axis_size("blk"))]


def stage_groups(low, high):
    return [
        [flat_index(base | member, mp, blk) for member in (0, low, high, low | high)]
        for mp, blk in columns()
        for base in range(lax.axis_size("dp"))
        if not base & (low | high)
    ]


def far_sum(part):
    count = lax.axis_size("dp")
    links = [
        [(flat_index(source, mp, blk), flat_index(source % 16, mp, blk)) for mp, blk in columns() for source in range(16 * run, 16 * run + 16)]
        for run in (1, 3, 2)
    ]
    total = part.astype(jnp.float32)
    for received in [lax.ppermute(part, axes, link) for link in links]:
        total += received.astype(jnp.float32)
    total = total.astype(jnp.bfloat16)
    returned = [lax.ppermute(total, axes, [(b, a) for a, b in link]) for link in links]
    shift = jnp.where(lax.axis_index("blk") % 2 == 0, core_shifts[0], core_shifts[1])
    first = (lax.axis_index("dp") // 2 - shift) % (count // 2) < 8
    return jnp.where(first, total, functools.reduce(jnp.add, returned))


def exchange(parts, groups):
    return lax.all_to_all(parts, axes, 0, 0, axis_index_groups=groups)


def summed(parts):
    return jnp.sum(parts.astype(jnp.float32), axis=0).astype(jnp.bfloat16)


def spread(part, groups):
    count = len(groups[0])
    return exchange(jnp.broadcast_to(part[None], (count,) + part.shape), groups)


def per_device(activations, cotangent):
    dp_count = lax.axis_size("dp")
    extent = cotangent.shape[1]
    slab_rows = extent // dp_count
    scaling = 1.0 / math.sqrt(activations.shape[0] * dp_count)
    near, middle = stage_groups(1, 2), stage_groups(4, 8)
    with jax.named_scope("product"):
        product = lax.dot_general(
            activations, cotangent, (((0,), (0,)), ((), ())), preferred_element_type=jnp.float32
        )
        part = (product * scaling).astype(jnp.bfloat16)
    with jax.named_scope("near_sum"):
        part = summed(exchange(part.reshape(4, extent // 4, extent), near))
    with jax.named_scope("middle_sum"):
        part = summed(exchange(part.reshape(4, extent // 16, extent), middle))
    with jax.named_scope("far_sum"):
        part = far_sum(part)
    with jax.named_scope("middle_gather"):
        part = spread(part, middle).reshape(extent // 4, extent)
    with jax.named_scope("near_gather"):
        gradient = spread(part, near).reshape(extent, extent)
    with jax.named_scope("precondition"):
        return jnp.transpose(precondition(gradient, slab_rows), (1, 0, 2))


def solution(mesh):
    placed = (P("dp", "blk"), P("dp", "mp"))
    return jax.shard_map(
        per_device, mesh=mesh, in_specs=placed, out_specs=P("blk", "dp", "mp"), check_vma=False
    )
```

```python
import functools
import math

import jax
import jax.numpy as jnp
import numpy as np
from jax import lax
from jax.experimental import pallas as pl
from jax.experimental.pallas import tpu as pltpu
from jax.sharding import PartitionSpec as P

ridge_shift = 0.05
tiny_shift = 1e-12
chunk = 640
axes = ("dp", "mp", "blk")
core_shifts = (0, 27)


def root_coefficients():
    poly = np.polynomial.Polynomial
    shifted = poly([ridge_shift, 1.0])
    factor = (5.0 - shifted) / 4.0
    return [float(c) for c in ((5.0 * factor - factor**5 * shifted) / 4.0).coef]


def folded(part):
    return jnp.sum(part.reshape(part.shape[0] // 8, 8, part.shape[1]), axis=0)


def precondition_kernel(
    g_ref, out_ref, stat, one, two, two_wide, three, mixed, base, wide, narrow, direction
):
    q = root_coefficients()
    extent = g_ref.shape[0]
    slices = [pl.ds(i * chunk, chunk) for i in range(extent // chunk)]

    def product(left, right):
        return jnp.dot(left, right, preferred_element_type=jnp.float32)

    total = jnp.zeros((8, extent), jnp.float32)
    for rows in slices:
        part = lax.dot_general(
            g_ref[:, rows], g_ref[...], (((0,), (0,)), ((), ())), preferred_element_type=jnp.float32
        )
        stat[rows, :] = part
        one[rows, :] = part.astype(jnp.bfloat16)
        total += folded(part * part)
    inverse = 1.0 / jnp.sqrt(jnp.sum(total) + tiny_shift)
    for rows in slices:
        part = product(one[rows, :], one[...]) * (inverse * inverse)
        two_wide[rows, :] = part
        two[rows, :] = part.astype(jnp.bfloat16)
    for rows in slices:
        cubed = product(one[rows, :], two[...]) * inverse
        first, second = stat[rows, :] * inverse, two_wide[rows, :]
        three[rows, :] = cubed.astype(jnp.bfloat16)
        base[rows, :] = q[1] * first + q[2] * second + q[3] * cubed
        mixed[rows, :] = (q[4] * first + q[5] * second + q[6] * cubed).astype(jnp.bfloat16)
    for rows in slices:
        part = base[rows, :] + product(three[rows, :], mixed[...])
        wide[rows, :] = part
        narrow[rows, :] = part.astype(jnp.bfloat16)
    for rows in slices:
        part = (2.0 * q[0]) * wide[rows, :] + product(narrow[rows, :], narrow[...])
        one[rows, :] = part.astype(jnp.bfloat16)
    gradient_norm = jnp.zeros((8, extent), jnp.float32)
    direction_norm = jnp.zeros((8, extent), jnp.float32)
    for rows in slices:
        widened = g_ref[rows, :].astype(jnp.float32)
        part = (q[0] * q[0]) * widened + product(g_ref[rows, :], one[...])
        direction[rows, :] = part
        gradient_norm += folded(widened * widened)
        direction_norm += folded(part * part)
    start = lax.axis_index("dp") * out_ref.shape[0]
    scale = jnp.sqrt(jnp.sum(gradient_norm) / (jnp.sum(direction_norm) + tiny_shift))
    for i in range(out_ref.shape[0]):
        out_ref[i] = direction[pl.ds(start + i, 1), :] * scale


def precondition(gradient, slab_rows):
    extent = gradient.shape[0]
    square = (extent, extent)
    f32, bf16 = pltpu.VMEM(square, jnp.float32), pltpu.VMEM(square, jnp.bfloat16)
    return pl.pallas_call(
        precondition_kernel,
        out_shape=jax.ShapeDtypeStruct((slab_rows, 1, extent), jnp.float32),
        in_specs=[
            pl.BlockSpec(memory_space=pltpu.VMEM),
        ],
        out_specs=pl.BlockSpec(memory_space=pltpu.VMEM),
        scratch_shapes=[f32, bf16, bf16, f32, bf16, bf16, f32, f32, bf16, f32],
        compiler_params=pltpu.CompilerParams(vmem_limit_bytes=40 * 1024 * 1024),
        cost_estimate=pl.CostEstimate(
            flops=12 * extent**3, bytes_accessed=2 * extent * extent, transcendentals=2
        ),
    )(gradient)


def flat_index(virtual, mp, blk):
    count, n_mp, n_blk = (lax.axis_size(axis) for axis in axes)
    place = (virtual // 2 + core_shifts[blk % 2]) % (count // 2) * 2 + virtual % 2
    return (place * n_mp + mp) * n_blk + blk


def columns():
    return [(mp, blk) for mp in range(lax.axis_size("mp")) for blk in range(lax.axis_size("blk"))]


def stage_groups(low, high):
    return [
        [flat_index(base | member, mp, blk) for member in (0, low, high, low | high)]
        for mp, blk in columns()
        for base in range(lax.axis_size("dp"))
        if not base & (low | high)
    ]


def far_sum(part):
    count = lax.axis_size("dp")
    links = [
        [(flat_index(source, mp, blk), flat_index(source % 16, mp, blk)) for mp, blk in columns() for source in range(16 * run, 16 * run + 16)]
        for run in (1, 3, 2)
    ]
    total = part.astype(jnp.float32)
    for received in [lax.ppermute(part, axes, link) for link in links]:
        total += received.astype(jnp.float32)
    total = total.astype(jnp.bfloat16)
    returned = [lax.ppermute(total, axes, [(b, a) for a, b in link]) for link in links[::-1]]
    shift = jnp.where(lax.axis_index("blk") % 2 == 0, core_shifts[0], core_shifts[1])
    first = (lax.axis_index("dp") // 2 - shift) % (count // 2) < 8
    return jnp.where(first, total, functools.reduce(jnp.add, returned))


def exchange(parts, groups):
    return lax.all_to_all(parts, axes, 0, 0, axis_index_groups=groups)


def summed(parts):
    return jnp.sum(parts.astype(jnp.float32), axis=0).astype(jnp.bfloat16)


def spread(part, groups):
    count = len(groups[0])
    return exchange(jnp.broadcast_to(part[None], (count,) + part.shape), groups)


def per_device(activations, cotangent):
    dp_count = lax.axis_size("dp")
    extent = cotangent.shape[1]
    slab_rows = extent // dp_count
    scaling = 1.0 / math.sqrt(activations.shape[0] * dp_count)
    near, middle = stage_groups(1, 2), stage_groups(4, 8)
    with jax.named_scope("product"):
        product = lax.dot_general(
            activations, cotangent, (((0,), (0,)), ((), ())), preferred_element_type=jnp.float32
        )
        part = (product * scaling).astype(jnp.bfloat16)
    with jax.named_scope("near_sum"):
        part = summed(exchange(part.reshape(4, extent // 4, extent), near))
    with jax.named_scope("middle_sum"):
        part = summed(exchange(part.reshape(4, extent // 16, extent), middle))
    with jax.named_scope("far_sum"):
        part = far_sum(part)
    with jax.named_scope("middle_gather"):
        part = spread(part, middle).reshape(extent // 4, extent)
    with jax.named_scope("near_gather"):
        gradient = spread(part, near).reshape(extent, extent)
    with jax.named_scope("precondition"):
        return jnp.transpose(precondition(gradient, slab_rows), (1, 0, 2))


def solution(mesh):
    placed = (P("dp", "blk"), P("dp", "mp"))
    return jax.shard_map(
        per_device, mesh=mesh, in_specs=placed, out_specs=P("blk", "dp", "mp"), check_vma=False
    )
```
